256 devices in a mesh: grp: 16 (over x, z_hi, core), sp: 16 (over y, z_lo).
Axes of the slice: x: 4, y: 4, z: 8 (z_hi: 2, z_lo: 4; z = z_hi * 4 + z_lo), core: 2. Of those that a mesh axis runs over, the one named last changes fastest.
Arguments:
- video: bfloat16 [16, 16, 128, 128, 128], P('grp', None, None, 'sp'), may hold values from -12 to 12
- cache: bfloat16 [16, 2, 128, 128, 128], P('grp', None, None, 'sp'), may hold values from -6 to 6
- conv_weight: bfloat16 [128, 3456], replicated, may hold values from -0.109375 to 0.109375
- latent_weight: bfloat16 [16, 128], replicated, may hold values from -0.5 to 0.5
- clip_lengths: int32 [16], replicated, may hold values from 1 to 16, as said below
Outputs:
- latents: bfloat16 [16, 16, 16, 128, 128], P('grp', None, None, 'sp')
The draws below stay inside these ranges and needn't reach their ends.
Inputs may be any that keep to these rules, and one draw needn't show every extreme that they name: `clip_lengths`: some clip has all 16 frames live and some clip a single one.
All inputs are finite; a program needn't handle non-finite values.
Results may differ from the reference program's by a relative error of at most 0.002.
Values may be sent and summed in bfloat16 or wider, within the bound.
No kernel may reach another device: no remote copies, remote signals or barrier semaphores. Data moves between devices by JAX's collectives and lax.ppermute only.
A program may use at most 128 MiB of HBM per device.

```python
import jax
import jax.numpy as jnp
from jax import lax

C = 128
LAT = 16
NORM_GROUPS = 32
W = 128
GROUPS = 16
FRAMES = 16
H = 128


def draw_video(key, part):
    key = jax.random.fold_in(key, 11)
    normals = jax.random.normal(key, (GROUPS, FRAMES, C, H, W), jnp.float32)
    row_pos = jnp.arange(H, dtype=jnp.float32)
    row_ramp = 1.0 + 2.0 * row_pos / max(H - 1, 1)
    values = normals * row_ramp[:, None]
    return jnp.clip(values, -12.0, 12.0).astype(jnp.bfloat16)


def draw_clip_lengths(key, part):
    key = jax.random.fold_in(key, 23)
    draw_key, order_key = jax.random.split(key)
    values = jax.random.randint(draw_key, (GROUPS,), 1, FRAMES + 1)
    order = jax.random.permutation(order_key, GROUPS)
    values = values.at[order[0]].set(FRAMES)
    values = values.at[order[1]].set(1)
    return values.astype(jnp.int32)


def block_scale(own_key, dims, cuts, low, largest):
    def one(position, blocks):
        heights = jax.random.uniform(jax.random.fold_in(jax.random.fold_in(own_key, 6), position), (blocks,), jnp.float32, low / len(cuts), largest / len(cuts))
        return jnp.repeat(jnp.exp(heights), dims[position] // blocks).reshape((-1,) + (1,) * (len(dims) - position - 1))

    gain = one(*cuts[0])
    for cut in cuts[1:]:
        gain = gain * one(*cut)
    return gain


def normal_values(stream_key, dims, scale, most, cuts=(), kind=jnp.bfloat16):
    values = jax.random.normal(stream_key, dims, jnp.float32) * scale
    if len(cuts) > 0:
        values = block_scale(stream_key, dims, cuts, -0.22, 0.18) * values
    return jnp.clip(values, min=-most, max=most).astype(kind)


def setup_inputs(seed: int = 0) -> dict:
    streams_of = jax.random.split(jax.random.key(seed), 6)
    video = draw_video(jax.random.fold_in(streams_of[5], 71), 0)
    cache = normal_values(streams_of[1], (GROUPS, 2, C, H, W), 1.0, 6.0, ((0, 16), (3, 16)))
    conv_weight = normal_values(streams_of[2], (C, 27 * C), (27 * C) ** -0.5, 0.109375)
    latent_weight = normal_values(streams_of[3], (LAT, C), C ** -0.5, 0.5)
    clip_lengths = draw_clip_lengths(jax.random.fold_in(streams_of[5], 71), 0)
    return {"video": video, "cache": cache, "conv_weight": conv_weight, "latent_weight": latent_weight, "clip_lengths": clip_lengths}


epsilon = 1e-06

def unfold(window, height, width):
    pieces = []
    for depth in range(3):
        for down in range(3):
            for across in range(3):
                pieces.append(window[depth, :, down:down + height, across:across + width])
    stacked = jnp.stack(pieces, 0)
    return stacked.reshape(27 * window.shape[1], height * width)

def clip_latents(clip, prior, length, conv_weight, latent_weight):
    frames, chans, height, width = clip.shape
    per_group = chans // NORM_GROUPS
    clip_f32 = clip.astype(jnp.float32)
    positions = jnp.arange(frames, dtype=jnp.int32)
    live_mask = (positions < length).astype(jnp.float32)
    grouped = clip_f32.reshape(frames, NORM_GROUPS, per_group, height, width)
    weights = live_mask[:, None, None, None, None]
    count = length.astype(jnp.float32) * (per_group * height * width)
    sums = lax.optimization_barrier(jnp.sum(grouped * weights, axis=(0, 2, 3, 4)))
    squares = lax.optimization_barrier(jnp.sum(grouped * grouped * weights, axis=(0, 2, 3, 4)))
    group_mean = sums / count
    variance = squares / count - group_mean * group_mean
    inverse = lax.rsqrt(variance + epsilon)
    normed = (grouped - group_mean[None, :, None, None, None]) * inverse[None, :, None, None, None]
    activated = jax.nn.silu(normed).reshape(frames, chans, height, width).astype(jnp.bfloat16)
    sequence = jnp.concatenate([prior, activated], 0)
    padded = jnp.pad(sequence, ((0, 0), (0, 0), (1, 1), (1, 1)))
    latent_f32 = latent_weight.astype(jnp.float32)

    def one_frame(frame_index):
        window = lax.dynamic_slice_in_dim(padded, frame_index, 3, 0)
        columns = unfold(window, height, width)
        conv_out = jnp.dot(conv_weight, columns, preferred_element_type=jnp.float32)
        own = lax.dynamic_index_in_dim(clip_f32, frame_index, 0, keepdims=False).reshape(chans, height * width)
        mixed = jax.nn.silu(own + conv_out)
        return jnp.dot(latent_f32, mixed, precision=lax.Precision.HIGHEST)
    result = lax.map(one_frame, positions)
    result = result * live_mask[:, None, None]
    return result.reshape(frames, latent_weight.shape[0], height, width).astype(jnp.bfloat16)

def reference(video, cache, conv_weight, latent_weight, clip_lengths):

    def per_clip(items):
        return clip_latents(items[0], items[1], items[2], conv_weight, latent_weight)
    return lax.map(per_clip, (video, cache, clip_lengths))
```

```python
import jax
import jax.numpy as jnp
from jax import lax
from jax.experimental import pallas as pl
from jax.experimental.pallas import tpu as pltpu
from jax.sharding import PartitionSpec as P

NORM_GROUPS = 32
epsilon = 1e-06
F32 = jnp.float32
BF16 = jnp.bfloat16


def half_silu(u):
    return u + u * jnp.tanh(u)


def stage_kernel(lengths_ref, video_ref, cache_ref, seq_ref, first_ref, last_ref, stats_ref, rows_ref, acc_ref):
    step = pl.program_id(0)
    frames, chans, height, width = video_ref.shape
    per_group = chans // NORM_GROUPS
    part = 16
    length = lengths_ref[lax.axis_index("grp")]

    @pl.when(step == 0)
    def _():
        acc_ref[...] = jnp.zeros_like(acc_ref)

    def turn(j, source, live):
        for k in range(chans // part):
            x = source[j, k * part : (k + 1) * part].astype(F32)
            rows_ref[j, k * part * height : (k + 1) * part * height] = x.reshape(part * height, width)
            if live is not None:
                some = slice(k * part // per_group, (k + 1) * part // per_group)
                grouped = x.reshape(part // per_group, per_group, height, width)
                acc_ref[0, some] += jnp.sum(grouped, axis=1) * live
                acc_ref[1, some] += jnp.sum(grouped * grouped, axis=1) * live
        for r in range(height):
            row = rows_ref[j, pl.ds(r, chans, stride=height), :].astype(BF16)
            seq_ref[j, r] = row
            if r == 0:
                first_ref[j] = row
            if r == height - 1:
                last_ref[j] = row

    @pl.when(step == 0)
    def _():
        for j in range(frames):
            turn(j, cache_ref, None)

    @pl.when(step > 0)
    def _():
        for j in range(frames):
            live = ((step - 1) * frames + j < length).astype(F32)
            turn(j, video_ref, live)

    @pl.when(step == pl.num_programs(0) - 1)
    def _():
        partial = jnp.sum(acc_ref[...], axis=2).reshape(2 * NORM_GROUPS, width)
        stats_ref[...] = lax.dot_general(
            jnp.ones((stats_ref.shape[0], width), F32), partial, (((1,), (1,)), ((), ())),
            precision=lax.Precision.HIGHEST, preferred_element_type=F32,
        )


def stage(lengths, video, cache):
    frames, chans, height, width = video.shape
    steps = frames // 2 + 1
    seq = frames + 2
    return pl.pallas_call(
        stage_kernel,
        grid=(steps,),
        in_specs=[
            pl.BlockSpec(memory_space=pltpu.SMEM),
            pl.BlockSpec((2, chans, height, width), lambda g: (jnp.maximum(g - 1, 0), 0, 0, 0)),
            pl.BlockSpec((2, chans, height, width), lambda g: (0, 0, 0, 0)),
        ],
        out_specs=[
            pl.BlockSpec((2, height, chans, width), lambda g: (g, 0, 0, 0)),
            pl.BlockSpec((2, chans, width), lambda g: (g, 0, 0)),
            pl.BlockSpec((2, chans, width), lambda g: (g, 0, 0)),
            pl.BlockSpec((8, 2 * NORM_GROUPS), lambda g: (0, 0)),
        ],
        out_shape=[
            jax.ShapeDtypeStruct((seq, height, chans, width), BF16),
            jax.ShapeDtypeStruct((seq, chans, width), BF16),
            jax.ShapeDtypeStruct((seq, chans, width), BF16),
            jax.ShapeDtypeStruct((8, 2 * NORM_GROUPS), F32),
        ],
        scratch_shapes=[
            pltpu.VMEM((2, chans * height, width), F32),
            pltpu.VMEM((2, NORM_GROUPS, height, width), F32),
        ],
        compiler_params=pltpu.CompilerParams(vmem_limit_bytes=32 * 1024 * 1024),
        cost_estimate=pl.CostEstimate(flops=10_000_000, bytes_accessed=10_600_000, transcendentals=0),
    )(lengths, pltpu.with_memory_space_constraint(video, pltpu.HBM), pltpu.with_memory_space_constraint(cache, pltpu.HBM))


def fill_norm(stats_ref, lengths_ref, norm_ref):
    _, chans, width = norm_ref.shape
    groups2 = stats_ref.shape[1]
    strips = lax.axis_size("sp")
    per_group = chans // NORM_GROUPS
    height = 8
    count = (lengths_ref[lax.axis_index("grp")] * (per_group * height * strips * width)).astype(F32)
    row = stats_ref[0:1, :] * jnp.ones((chans, 1), F32) / count
    lane = lax.broadcasted_iota(jnp.int32, (chans, groups2), 1)
    group = lax.broadcasted_iota(jnp.int32, (chans, groups2), 0) // per_group
    mean = jnp.sum(jnp.where(lane == group, row, 0.0), axis=1, keepdims=True)
    square = jnp.sum(jnp.where(lane == group + NORM_GROUPS, row, 0.0), axis=1, keepdims=True)
    scale = 0.5 * lax.rsqrt(square - mean * mean + epsilon)
    norm_ref[0] = jnp.broadcast_to(scale, (chans, width))
    norm_ref[1] = jnp.broadcast_to(-mean * scale, (chans, width))


def fill_weight(raw_ref, weight_ref, taps):
    chans = raw_ref.shape[0]
    for i, b in enumerate(taps):
        for a in range(3):
            for e in range(3):
                source = ((a * 3 + b) * 3 + e) * chans
                column = (i * 3 + a) * chans
                weight_ref[e * chans : (e + 1) * chans, column : column + chans] = raw_ref[:, source : source + chans]


def shift_sum(y, chans, width):
    outs = []
    lane = lax.broadcasted_iota(jnp.int32, (chans, width), 1)
    for f in range(y.shape[1] // width):
        part = slice(f * width, (f + 1) * width)
        left = pltpu.roll(y[0:chans, part], 1, 1)
        right = pltpu.roll(y[2 * chans : 3 * chans, part], width - 1, 1)
        outs.append(
            y[chans : 2 * chans, part] + jnp.where(lane > 0, left, 0.0) + jnp.where(lane < width - 1, right, 0.0)
        )
    return outs


def project(latent, mixed):
    latent2 = jnp.concatenate([latent, latent], axis=1)
    value = jnp.concatenate(mixed, axis=1)
    high = value.astype(BF16)
    low = (value - high.astype(F32)).astype(BF16)
    return jnp.dot(latent2, jnp.concatenate([high, low], axis=0), preferred_element_type=F32)


def conv_kernel(
    lengths_ref, stats_ref, next_ref, own_ref, raw_ref, latent_ref, lat_ref, edge_ref,
    norm_ref, weight_ref, held_ref, ahead_ref,
):
    step = pl.program_id(0)
    pair, height, chans, width = own_ref.shape

    def activate(r):
        for j in range(pair):
            u = next_ref[j, r].astype(F32) * norm_ref[0] + norm_ref[1]
            ahead_ref[j, r] = half_silu(u).astype(BF16)

    @pl.when(step == 0)
    def _():
        fill_norm(stats_ref, lengths_ref, norm_ref)
        fill_weight(raw_ref, weight_ref, range(3))
        held_ref[0] = own_ref[...]
        for r in range(height):
            activate(r)

    @pl.when(step > 0)
    def _():
        before = (step - 1) % 2
        now = step % 2
        held_ref[now] = ahead_ref[...]
        deep = 3 * chans

        def taps_of(r):
            return [b for b in range(3) if 0 <= r + b - 1 < height]

        def multiply(rows):
            taps = taps_of(rows[0])
            columns = []
            for r in rows:
                for f in range(pair):
                    blocks = []
                    for b in taps:
                        for a in range(3):
                            slot = before if f + a < 2 else now
                            blocks.append(held_ref[slot, (f + a) % 2, r + b - 1])
                    columns.append(jnp.concatenate(blocks, axis=0))
            x = jnp.concatenate(columns, axis=1)
            return jnp.dot(weight_ref[:, taps[0] * deep : (taps[-1] + 1) * deep], x, preferred_element_type=F32)

        def mix(rows, y):
            conv = shift_sum(y, chans, width)
            places = [(r, f) for r in rows for f in range(pair)]
            mixed = [conv[i] + own_ref[f, r].astype(F32) for i, (r, f) in enumerate(places)]
            if rows[0] == 0 or rows[0] == height - 1:
                for m, (r, f) in zip(mixed, places):
                    edge_ref[f, 0 if r == 0 else 1] = m
                return None
            return [half_silu(0.5 * m) for m in mixed]

        def write(rows, mixed):
            latent = project(latent_ref[...], mixed)
            places = [(r, f) for r in rows for f in range(pair)]
            for i, (r, f) in enumerate(places):
                lat_ref[f, pl.ds(r, latent.shape[0], stride=height), :] = latent[:, i * width : (i + 1) * width]

        order = [list(range(1, 4)), list(range(4, 7)), [0], [height - 1]]
        todo_mix, todo_write = [], []
        todo_act = list(range(height))
        for rows in order:
            y = multiply(rows)
            if todo_mix:
                prev, py = todo_mix.pop(0)
                mixed = mix(prev, py)
                if mixed is not None:
                    todo_write.append((prev, mixed))
            for _ in range(-(-height // len(order))):
                if todo_act:
                    activate(todo_act.pop(0))
            if len(todo_write) > 1:
                write(*todo_write.pop(0))
            todo_mix.append((rows, y))
        for prev, py in todo_mix:
            mixed = mix(prev, py)
            if mixed is not None:
                todo_write.append((prev, mixed))
        for item in todo_write:
            write(*item)


def convolve(lengths, stats, seq, weight, latent):
    total, height, chans, width = seq.shape
    frames = total - 2
    lat = latent.shape[0]
    pairs = total // 2
    back = lambda g: jnp.maximum(g - 1, 0)
    return pl.pallas_call(
        conv_kernel,
        grid=(pairs,),
        in_specs=[
            pl.BlockSpec(memory_space=pltpu.SMEM),
            pl.BlockSpec(stats.shape, lambda g: (0, 0)),
            pl.BlockSpec((2, height, chans, width), lambda g: (jnp.minimum(g + 1, pairs - 1), 0, 0, 0)),
            pl.BlockSpec((2, height, chans, width), lambda g: (g, 0, 0, 0)),
            pl.BlockSpec(weight.shape, lambda g: (0, 0)),
            pl.BlockSpec(latent.shape, lambda g: (0, 0)),
        ],
        out_specs=[
            pl.BlockSpec((2, lat * height, width), lambda g: (back(g), 0, 0)),
            pl.BlockSpec((2, 2, chans, width), lambda g: (back(g), 0, 0, 0)),
        ],
        out_shape=[
            jax.ShapeDtypeStruct((frames, lat * height, width), F32),
            jax.ShapeDtypeStruct((frames, 2, chans, width), F32),
        ],
        scratch_shapes=[
            pltpu.VMEM((2, chans, width), F32),
            pltpu.VMEM((3 * chans, 9 * chans), BF16),
            pltpu.VMEM((2, 2, height, chans, width), BF16),
            pltpu.VMEM((2, height, chans, width), BF16),
        ],
        compiler_params=pltpu.CompilerParams(vmem_limit_bytes=24 * 1024 * 1024),
        cost_estimate=pl.CostEstimate(flops=1_000_000_000, bytes_accessed=1_000_000, transcendentals=1_000_000),
    )(lengths, stats, seq, seq, weight, latent)


def finish_kernel(
    lengths_ref, stats_ref, above_ref, below_ref, raw_ref, latent_ref, lat_ref, edge_ref, out_ref,
    norm_ref, weight_ref, halo_ref, rows_ref,
):
    frames, lat, height, width = out_ref.shape
    total, chans, _ = above_ref.shape
    deep = 3 * chans
    length = lengths_ref[lax.axis_index("grp")]
    strip = lax.axis_index("sp")
    inside = ((strip > 0).astype(F32), (strip < lax.axis_size("sp") - 1).astype(F32))
    halos = (above_ref, below_ref)
    fill_norm(stats_ref, lengths_ref, norm_ref)
    fill_weight(raw_ref, weight_ref, (0, 2))

    def activate(t):
        for side in range(2):
            value = halos[side][t].astype(F32)
            if t >= 2:
                value = half_silu(value * norm_ref[0] + norm_ref[1])
            halo_ref[side, t] = (value * inside[side]).astype(BF16)

    def multiply(side, p):
        columns = [jnp.concatenate([halo_ref[side, 2 * p + f + a] for a in range(3)], axis=0) for f in range(2)]
        return jnp.dot(
            weight_ref[:, side * deep : (side + 1) * deep], jnp.concatenate(columns, axis=1), preferred_element_type=F32
        )

    def mix(side, p, y):
        conv = shift_sum(y, chans, width)
        return [half_silu(0.5 * (conv[f] + edge_ref[2 * p + f, side])) for f in range(2)]

    def write(side, p, mixed):
        latent = project(latent_ref[...], mixed)
        for f in range(2):
            rows_ref[2 * p + f, pl.ds(side * (height - 1), lat, stride=height), :] = latent[:, f * width : (f + 1) * width]

    def put(p):
        for t in (2 * p, 2 * p + 1):
            live = (t < length).astype(F32)
            out_ref[t] = (rows_ref[t] * live).reshape(lat, height, width).astype(BF16)

    for t in range(4):
        activate(t)
    to_mix, to_write = [], []
    for p in range(frames // 2):
        for side in range(2):
            y = multiply(side, p)
            if side == 0:
                rows_ref[2 * p : 2 * p + 2] = lat_ref[2 * p : 2 * p + 2]
                if 2 * p + 4 < total:
                    activate(2 * p + 4)
            elif 2 * p + 5 < total:
                activate(2 * p + 5)
            if to_mix:
                before = to_mix.pop(0)
                to_write.append(before[:2] + (mix(*before),))
            if len(to_write) > 1:
                done = to_write.pop(0)
                write(*done)
                if done[0] == 1:
                    put(done[1])
            to_mix.append((side, p, y))
    for item in to_mix:
        to_write.append(item[:2] + (mix(*item),))
    for item in to_write:
        write(*item)
        if item[0] == 1:
            put(item[1])


def finish(lengths, stats, above, below, weight, latent, lat_rows, edge, height):
    total, chans, width = above.shape
    frames = total - 2
    lat = latent.shape[0]
    vmem = pl.BlockSpec(memory_space=pltpu.VMEM)
    return pl.pallas_call(
        finish_kernel,
        in_specs=[pl.BlockSpec(memory_space=pltpu.SMEM)] + [vmem] * 7,
        out_specs=vmem,
        out_shape=jax.ShapeDtypeStruct((frames, lat, height, width), BF16),
        scratch_shapes=[
            pltpu.VMEM((2, chans, width), F32),
            pltpu.VMEM((3 * chans, 6 * chans), BF16),
            pltpu.VMEM((2, total, chans, width), BF16),
            pltpu.VMEM((frames, lat * height, width), F32),
        ],
        compiler_params=pltpu.CompilerParams(vmem_limit_bytes=24 * 1024 * 1024),
        cost_estimate=pl.CostEstimate(flops=1_300_000_000, bytes_accessed=6_000_000, transcendentals=1_000_000),
    )(lengths, stats, above, below, weight, latent, lat_rows, edge)


def body(video, cache, conv_weight, latent_weight, clip_lengths):
    clip = video[0]
    prior = cache[0]
    height = clip.shape[2]
    strips = lax.axis_size("sp")
    seq, first, last, stats = stage(clip_lengths, clip, prior)

    def meet(value, hop):
        return value + lax.ppermute(value, "sp", [(i, i ^ hop) for i in range(strips)])

    stats = meet(meet(stats, 1), 2)
    stats, first, last = lax.optimization_barrier((stats, first, last))
    above = lax.ppermute(last, "sp", [(i, i + 1) for i in range(strips - 1)])
    below = lax.ppermute(first, "sp", [(i + 1, i) for i in range(strips - 1)])
    stats = meet(meet(stats, 4), 8)
    lat_rows, edge = convolve(clip_lengths, stats, seq, conv_weight, latent_weight)
    out = finish(clip_lengths, stats, above, below, conv_weight, latent_weight, lat_rows, edge, height)
    return out[None]


def solution(mesh):
    in_specs = (P("grp", None, None, "sp", None), P("grp", None, None, "sp", None), P(), P(), P())
    out_specs = P("grp", None, None, "sp", None)
    return jax.shard_map(body, mesh=mesh, in_specs=in_specs, out_specs=out_specs, check_vma=False)
```

```python
import functools

import jax
import jax.numpy as jnp
from jax import lax
from jax.experimental import pallas as pl
from jax.experimental.pallas import tpu as pltpu
from jax.sharding import PartitionSpec as P

NORM_GROUPS = 32
epsilon = 1e-06
F32 = jnp.float32
BF16 = jnp.bfloat16


def half_silu(u):
    return u + u * jnp.tanh(u)


def stage_kernel(
    lengths_ref, video_ref, cache_ref, first_out_ref, last_out_ref, stats_ref,
    held_ref, rows_ref, acc_ref, first_ref, last_ref, sems, out_sems,
):
    total, chans, width = first_ref.shape
    height = video_ref.shape[1] // chans
    per_group = chans // NORM_GROUPS
    part = 16
    length = lengths_ref[lax.axis_index("grp")]

    def fetch(p):
        return pltpu.make_async_copy(video_ref.at[pl.ds(2 * p - 2, 2)], held_ref.at[pl.ds(2 * p, 2)], sems.at[p])

    def fetch_cache():
        return pltpu.make_async_copy(cache_ref, held_ref.at[pl.ds(0, 2)], sems.at[0])

    def leave(p, part):
        held, out = ((first_ref, first_out_ref), (last_ref, last_out_ref))[part]
        return pltpu.make_async_copy(held.at[pl.ds(2 * p, 2)], out.at[pl.ds(2 * p, 2)], out_sems.at[p, part])

    for p in range(1, total // 2):
        fetch(p).start()
    fetch_cache().start()
    acc_ref[...] = jnp.zeros_like(acc_ref)

    def turn(j, t, live):
        for k in range(chans // part):
            rows = slice(k * part * height, (k + 1) * part * height)
            x = held_ref[t, rows].astype(F32)
            rows_ref[j, rows] = x
            if live is not None:
                some = slice(k * part // per_group, (k + 1) * part // per_group)
                grouped = x.reshape(part // per_group, per_group, height, width)
                acc_ref[0, some] += jnp.sum(grouped, axis=1) * live
                acc_ref[1, some] += jnp.sum(grouped * grouped, axis=1) * live
        first_ref[t] = rows_ref[j, pl.ds(0, chans, stride=height), :].astype(BF16)
        last_ref[t] = rows_ref[j, pl.ds(height - 1, chans, stride=height), :].astype(BF16)

    def pair(p, carry):
        fetch(p).wait()
        for j in range(2):
            turn(j, 2 * p + j, (2 * p - 2 + j < length).astype(F32))
        for part in range(2):
            leave(p, part).start()
        return carry

    lax.fori_loop(1, total // 2, pair, 0)
    fetch_cache().wait()
    for j in range(2):
        turn(j, j, None)
    for part in range(2):
        leave(0, part).start()
    partial = jnp.sum(acc_ref[...], axis=2).reshape(2 * NORM_GROUPS, width)
    stats_ref[...] = lax.dot_general(
        jnp.ones((stats_ref.shape[0], width), F32), partial, (((1,), (1,)), ((), ())),
        precision=lax.Precision.HIGHEST, preferred_element_type=F32,
    )
    for p in range(total // 2):
        for part in range(2):
            leave(p, part).wait()


def stage(lengths, video, cache, chans, copies):
    frames, rows, width = video.shape
    total = frames + 2
    vmem = pl.BlockSpec(memory_space=pltpu.VMEM)
    hbm = pl.BlockSpec(memory_space=pl.ANY)
    return pl.pallas_call(
        stage_kernel,
        in_specs=[pl.BlockSpec(memory_space=pltpu.SMEM), hbm, hbm],
        out_specs=[hbm, hbm, vmem],
        out_shape=[
            pltpu.HBM((total, chans, width), BF16),
            pltpu.HBM((total, chans, width), BF16),
            jax.ShapeDtypeStruct((copies, 2 * NORM_GROUPS), F32),
        ],
        scratch_shapes=[
            pltpu.VMEM((total, rows, width), BF16),
            pltpu.VMEM((2, rows, width), F32),
            pltpu.VMEM((2, NORM_GROUPS, rows // chans, width), F32),
            pltpu.VMEM((total, chans, width), BF16),
            pltpu.VMEM((total, chans, width), BF16),
            pltpu.SemaphoreType.DMA((total // 2,)),
            pltpu.SemaphoreType.DMA((total // 2, 2)),
        ],
        compiler_params=pltpu.CompilerParams(vmem_limit_bytes=20 * 1024 * 1024),
        cost_estimate=pl.CostEstimate(flops=10_000_000, bytes_accessed=5_000_000, transcendentals=0),
    )(lengths, in_hbm(video), in_hbm(cache))


def in_hbm(value):
    return pltpu.with_memory_space_constraint(value, pltpu.HBM)


def prepare_kernel(first_in_ref, last_in_ref, raw_ref, first_ref, last_ref, weight_ref):
    chans = raw_ref.shape[0]
    for b in range(3):
        for a in range(3):
            for e in range(3):
                source = ((a * 3 + b) * 3 + e) * chans
                column = (b * 3 + a) * chans
                weight_ref[e * chans : (e + 1) * chans, column : column + chans] = raw_ref[:, source : source + chans]


def prepare(first, last, weight):
    chans = weight.shape[0]
    vmem = pl.BlockSpec(memory_space=pltpu.VMEM)
    hbm = pl.BlockSpec(memory_space=pl.ANY)
    return pl.pallas_call(
        prepare_kernel,
        in_specs=[hbm, hbm, vmem],
        out_specs=[hbm, hbm, vmem],
        out_shape=[
            pltpu.HBM(first.shape, BF16),
            pltpu.HBM(last.shape, BF16),
            jax.ShapeDtypeStruct((3 * chans, 9 * chans), BF16),
        ],
        input_output_aliases={0: 0, 1: 1},
        compiler_params=pltpu.CompilerParams(vmem_limit_bytes=16 * 1024 * 1024),
        cost_estimate=pl.CostEstimate(flops=6_000_000_000, bytes_accessed=20_000_000, transcendentals=0),
    )(in_hbm(first), in_hbm(last), weight)


def fill_norm(stats_ref, lengths_ref, norm_ref):
    _, chans, width = norm_ref.shape
    strips, groups2 = stats_ref.shape
    per_group = chans // NORM_GROUPS
    height = 8
    count = (lengths_ref[lax.axis_index("grp")] * (per_group * height * strips * width)).astype(F32)
    row = jnp.sum(stats_ref[...], axis=0, keepdims=True) * jnp.ones((chans, 1), F32) / count
    lane = lax.broadcasted_iota(jnp.int32, (chans, groups2), 1)
    group = lax.broadcasted_iota(jnp.int32, (chans, groups2), 0) // per_group
    mean = jnp.sum(jnp.where(lane == group, row, 0.0), axis=1, keepdims=True)
    square = jnp.sum(jnp.where(lane == group + NORM_GROUPS, row, 0.0), axis=1, keepdims=True)
    scale = 0.5 * lax.rsqrt(square - mean * mean + epsilon)
    norm_ref[0] = jnp.broadcast_to(scale, (chans, width))
    norm_ref[1] = jnp.broadcast_to(-mean * scale, (chans, width))


def shift_sum(y, chans, width):
    outs = []
    lane = lax.broadcasted_iota(jnp.int32, (chans, width), 1)
    for f in range(y.shape[1] // width):
        part = slice(f * width, (f + 1) * width)
        left = pltpu.roll(y[0:chans, part], 1, 1)
        right = pltpu.roll(y[2 * chans : 3 * chans, part], width - 1, 1)
        outs.append(
            y[chans : 2 * chans, part] + jnp.where(lane > 0, left, 0.0) + jnp.where(lane < width - 1, right, 0.0)
        )
    return outs


def project(latent, mixed):
    latent2 = jnp.concatenate([latent, latent], axis=1)
    value = jnp.concatenate(mixed, axis=1)
    high = value.astype(BF16)
    low = (value - high.astype(F32)).astype(BF16)
    return jnp.dot(latent2, jnp.concatenate([high, low], axis=0), preferred_element_type=F32)


def conv_kernel(
    lengths_ref, stats_ref, video_ref, cache_ref, weight_ref, latent_ref, lat_ref, edge_ref,
    seq_ref, rows_ref, norm_ref, sems, *buffers,
):
    pair, height, chans, width = buffers[0].shape
    total = seq_ref.shape[0]
    pairs = total // 2
    held, owns = buffers[:3], buffers[3:]
    deep = 3 * chans
    order = [list(range(1, 4)), list(range(4, 7)), [0], [height - 1]]

    def fetch(p):
        return pltpu.make_async_copy(video_ref.at[pl.ds(2 * p - 2, 2)], seq_ref.at[pl.ds(2 * p, 2)], sems.at[p])

    def fetch_cache():
        return pltpu.make_async_copy(cache_ref, seq_ref.at[pl.ds(0, 2)], sems.at[0])

    fetch_cache().start()
    for p in range(1, pairs):
        fetch(p).start()
    fill_norm(stats_ref, lengths_ref, norm_ref)

    def widen(p):
        for j in range(pair):
            rows_ref[j] = seq_ref[2 * p + j].astype(F32)

    def turn(j, r):
        return rows_ref[j, pl.ds(r, chans, stride=height), :]

    def activate(k, r):
        for j in range(pair):
            x = turn(j, r)
            owns[k % 3][j, r] = x.astype(BF16)
            held[k % 3][j, r] = half_silu(x * norm_ref[0] + norm_ref[1]).astype(BF16)

    fetch_cache().wait()
    widen(0)
    for r in range(height):
        for j in range(pair):
            held[0][j, r] = turn(j, r).astype(BF16)
    fetch(1).wait()
    widen(1)
    for r in range(height):
        activate(1, r)

    def taps_of(r):
        return [b for b in range(3) if 0 <= r + b - 1 < height]

    def step(p, k, more):
        before, now, own_ref = held[(k - 1) % 3], held[k % 3], owns[k % 3]
        if more:
            fetch(p + 1).wait()
            widen(p + 1)

        def multiply(rows):
            taps = taps_of(rows[0])
            columns = []
            for r in rows:
                for f in range(pair):
                    blocks = []
                    for b in taps:
                        for a in range(3):
                            source = before if f + a < 2 else now
                            blocks.append(source[(f + a) % 2, r + b - 1])
                    columns.append(jnp.concatenate(blocks, axis=0))
            x = jnp.concatenate(columns, axis=1)
            return jnp.dot(weight_ref[:, taps[0] * deep : (taps[-1] + 1) * deep], x, preferred_element_type=F32)

        def mix(rows, y):
            conv = shift_sum(y, chans, width)
            places = [(r, f) for r in rows for f in range(pair)]
            mixed = [conv[i] + own_ref[f, r].astype(F32) for i, (r, f) in enumerate(places)]
            if rows[0] == 0 or rows[0] == height - 1:
                for m, (r, f) in zip(mixed, places):
                    edge_ref[2 * p - 2 + f, 0 if r == 0 else 1] = m
                return None
            return [half_silu(0.5 * m) for m in mixed]

        def write(rows, mixed):
            latent = project(latent_ref[...], mixed)
            places = [(r, f) for r in rows for f in range(pair)]
            for i, (r, f) in enumerate(places):
                lat_ref[2 * p - 2 + f, pl.ds(r, latent.shape[0], stride=height), :] = latent[:, i * width : (i + 1) * width]

        to_mix, to_write = [], []
        to_activate = list(range(height)) if more else []
        for rows in order:
            y = multiply(rows)
            if to_mix:
                done, its = to_mix.pop(0)
                mixed = mix(done, its)
                if mixed is not None:
                    to_write.append((done, mixed))
            for _ in range(-(-height // len(order))):
                if to_activate:
                    activate(k + 1, to_activate.pop(0))
            if len(to_write) > 1:
                write(*to_write.pop(0))
            to_mix.append((rows, y))
        for done, its in to_mix:
            mixed = mix(done, its)
            if mixed is not None:
                to_write.append((done, mixed))
        for item in to_write:
            write(*item)

    def steps(i, carry):
        for k in range(1, 4):
            step(3 * i + k, k, True)
        return carry

    turns = (pairs - 2) // 3
    lax.fori_loop(0, turns, steps, 0)
    for p in range(3 * turns + 1, pairs):
        step(p, p, p + 1 < pairs)


def convolve(lengths, stats, video, cache, weight, latent):
    frames, rows, width = video.shape
    chans = weight.shape[0] // 3
    height = rows // chans
    total = frames + 2
    lat = latent.shape[0]
    vmem = pl.BlockSpec(memory_space=pltpu.VMEM)
    hbm = pl.BlockSpec(memory_space=pl.ANY)
    return pl.pallas_call(
        conv_kernel,
        in_specs=[pl.BlockSpec(memory_space=pltpu.SMEM), vmem, hbm, hbm, vmem, vmem],
        out_specs=[vmem, vmem],
        out_shape=[
            jax.ShapeDtypeStruct((frames, lat * height, width), F32),
            jax.ShapeDtypeStruct((frames, 2, chans, width), F32),
        ],
        scratch_shapes=[
            pltpu.VMEM((total, rows, width), BF16),
            pltpu.VMEM((2, rows, width), F32),
            pltpu.VMEM((2, chans, width), F32),
            pltpu.SemaphoreType.DMA((total // 2,)),
        ]
        + [pltpu.VMEM((2, height, chans, width), BF16)] * 6,
        compiler_params=pltpu.CompilerParams(vmem_limit_bytes=24 * 1024 * 1024),
        cost_estimate=pl.CostEstimate(flops=13_000_000_000, bytes_accessed=14_000_000, transcendentals=4_000_000),
    )(lengths, stats, in_hbm(video), in_hbm(cache), weight, latent)


def finish_kernel(
    side, final, lengths_ref, stats_ref, row_ref, weight_ref, latent_ref, lat_ref, edge_ref, out_ref,
    norm_ref, halo_ref, *scratch,
):
    total, chans, width = row_ref.shape
    frames = total - 2
    lat = latent_ref.shape[0]
    height = lat_ref.shape[1] // lat
    deep = 3 * chans
    length = lengths_ref[lax.axis_index("grp")]
    strip = lax.axis_index("sp")
    inside = (strip < lax.axis_size("sp") - 1 if side else strip > 0).astype(F32)
    fill_norm(stats_ref, lengths_ref, norm_ref)

    def activate(t):
        value = row_ref[t].astype(F32)
        if t >= 2:
            value = half_silu(value * norm_ref[0] + norm_ref[1])
        halo_ref[t] = (value * inside).astype(BF16)

    def multiply(p):
        columns = [jnp.concatenate([halo_ref[2 * p + f + a] for a in range(3)], axis=0) for f in range(2)]
        return jnp.dot(
            weight_ref[:, 2 * side * deep : (2 * side + 1) * deep], jnp.concatenate(columns, axis=1), preferred_element_type=F32
        )

    def mix(p, y):
        conv = shift_sum(y, chans, width)
        return [half_silu(0.5 * (conv[f] + edge_ref[2 * p + f, side])) for f in range(2)]

    def write(p, mixed):
        latent = project(latent_ref[...], mixed)
        rows_ref = scratch[0] if final else out_ref
        for f in range(2):
            t = 2 * p + f
            rows_ref[t, pl.ds(side * (height - 1), lat, stride=height), :] = latent[:, f * width : (f + 1) * width]
            if final:
                live = (t < length).astype(F32)
                out_ref[t] = (rows_ref[t] * live).reshape(lat, height, width).astype(BF16)

    if final:
        scratch[0][...] = lat_ref[...]
    else:
        out_ref[...] = lat_ref[...]
    for t in range(4):
        activate(t)
    to_mix, to_write = [], []
    for p in range(frames // 2):
        y = multiply(p)
        for t in (2 * p + 4, 2 * p + 5):
            if t < total:
                activate(t)
        if to_mix:
            before = to_mix.pop(0)
            to_write.append((before[0], mix(*before)))
        if len(to_write) > 1:
            write(*to_write.pop(0))
        to_mix.append((p, y))
    for item in to_mix:
        to_write.append((item[0], mix(*item)))
    for item in to_write:
        write(*item)


def finish(side, final, lengths, stats, row, weight, latent, lat_rows, edge):
    total, chans, width = row.shape
    frames = total - 2
    lat = latent.shape[0]
    height = lat_rows.shape[1] // lat
    vmem = pl.BlockSpec(memory_space=pltpu.VMEM)
    scratch = [pltpu.VMEM((2, chans, width), F32), pltpu.VMEM((total, chans, width), BF16)]
    if final:
        out = jax.ShapeDtypeStruct((frames, lat, height, width), BF16)
        scratch.append(pltpu.VMEM(lat_rows.shape, F32))
    else:
        out = jax.ShapeDtypeStruct(lat_rows.shape, F32)
    return pl.pallas_call(
        functools.partial(finish_kernel, side, final),
        in_specs=[pl.BlockSpec(memory_space=pltpu.SMEM)] + [vmem] * 6,
        out_specs=vmem,
        out_shape=out,
        scratch_shapes=scratch,
        compiler_params=pltpu.CompilerParams(vmem_limit_bytes=20 * 1024 * 1024),
        cost_estimate=pl.CostEstimate(flops=700_000_000, bytes_accessed=3_000_000, transcendentals=500_000),
    )(lengths, stats, row, weight, latent, lat_rows, edge)


def body(video, cache, conv_weight, latent_weight, clip_lengths):
    _, frames, chans, height, width = video.shape
    video = video.reshape(frames, chans * height, width)
    cache = cache.reshape(2, chans * height, width)
    strips = lax.axis_size("sp")
    first, last, stats = stage(clip_lengths, video, cache, chans, strips)
    stats = lax.all_to_all(stats, "sp", split_axis=0, concat_axis=0, tiled=True)
    first, last, weight = prepare(first, last, conv_weight)
    above = lax.ppermute(last, "sp", [(i, i + 1) for i in range(strips - 1)])
    below = lax.ppermute(first, "sp", [(i + 1, i) for i in range(strips - 1)])
    lat_rows, edge = convolve(clip_lengths, stats, video, cache, weight, latent_weight)
    lat_rows = finish(0, False, clip_lengths, stats, above, weight, latent_weight, lat_rows, edge)
    out = finish(1, True, clip_lengths, stats, below, weight, latent_weight, lat_rows, edge)
    return out[None]


def solution(mesh):
    in_specs = (P("grp", None, None, "sp", None), P("grp", None, None, "sp", None), P(), P(), P())
    out_specs = P("grp", None, None, "sp", None)
    return jax.shard_map(body, mesh=mesh, in_specs=in_specs, out_specs=out_specs, check_vma=False)
```

```python
import functools

import jax
import jax.numpy as jnp
from jax import lax
from jax.experimental import pallas as pl
from jax.experimental.pallas import tpu as pltpu
from jax.sharding import PartitionSpec as P

NORM_GROUPS = 32
epsilon = 1e-06
F32 = jnp.float32
BF16 = jnp.bfloat16


def half_silu(u):
    return u + u * jnp.tanh(u)


def stage_kernel(
    lengths_ref, video_ref, cache_ref, first_out_ref, last_out_ref, stats_ref,
    held_ref, rows_ref, acc_ref, first_ref, last_ref, table_ref, sems, out_sems, table_sem,
):
    total, chans, width = first_ref.shape
    height = video_ref.shape[1] // chans
    per_group = chans // NORM_GROUPS
    part = 16
    table = pltpu.make_async_copy(lengths_ref, table_ref, table_sem)
    table.start()

    def fetch(p):
        return pltpu.make_async_copy(video_ref.at[pl.ds(2 * p - 2, 2)], held_ref.at[pl.ds(2 * p, 2)], sems.at[p])

    def fetch_cache():
        return pltpu.make_async_copy(cache_ref, held_ref.at[pl.ds(0, 2)], sems.at[0])

    def leave(p, side):
        held, out = ((first_ref, first_out_ref), (last_ref, last_out_ref))[side]
        return pltpu.make_async_copy(held.at[pl.ds(2 * p, 2)], out.at[pl.ds(2 * p, 2)], out_sems.at[p, side])

    for p in range(1, total // 2):
        fetch(p).start()
    fetch_cache().start()
    acc_ref[...] = jnp.zeros_like(acc_ref)
    table.wait()
    length = table_ref[lax.axis_index("grp")]

    def turn(j, t, live):
        for k in range(chans // part):
            rows = slice(k * part * height, (k + 1) * part * height)
            x = held_ref[t, rows].astype(F32)
            rows_ref[j, rows] = x
            if live is not None:
                some = slice(k * part // per_group, (k + 1) * part // per_group)
                grouped = x.reshape(part // per_group, per_group, height, width)
                acc_ref[0, some] += jnp.sum(grouped, axis=1) * live
                acc_ref[1, some] += jnp.sum(grouped * grouped, axis=1) * live
        first_ref[t] = rows_ref[j, pl.ds(0, chans, stride=height), :].astype(BF16)
        last_ref[t] = rows_ref[j, pl.ds(height - 1, chans, stride=height), :].astype(BF16)

    def pair(p, carry):
        fetch(p).wait()
        for j in range(2):
            turn(j, 2 * p + j, (2 * p - 2 + j < length).astype(F32))
        for side in range(2):
            leave(p, side).start()
        return carry

    lax.fori_loop(1, total // 2, pair, 0)
    fetch_cache().wait()
    for j in range(2):
        turn(j, j, None)
    for side in range(2):
        leave(0, side).start()
    partial = jnp.sum(acc_ref[...], axis=2).reshape(2 * NORM_GROUPS, width)
    stats_ref[...] = lax.dot_general(
        jnp.ones((stats_ref.shape[0], width), F32), partial, (((1,), (1,)), ((), ())),
        precision=lax.Precision.HIGHEST, preferred_element_type=F32,
    )
    for p in range(total // 2):
        for side in range(2):
            leave(p, side).wait()


def stage(lengths, video, cache, chans, copies):
    frames, rows, width = video.shape
    total = frames + 2
    vmem = pl.BlockSpec(memory_space=pltpu.VMEM)
    hbm = pl.BlockSpec(memory_space=pl.ANY)
    return pl.pallas_call(
        stage_kernel,
        in_specs=[hbm, hbm, hbm],
        out_specs=[hbm, hbm, vmem],
        out_shape=[
            pltpu.HBM((total, chans, width), BF16),
            pltpu.HBM((total, chans, width), BF16),
            jax.ShapeDtypeStruct((copies, 2 * NORM_GROUPS), F32),
        ],
        scratch_shapes=[
            pltpu.VMEM((total, rows, width), BF16),
            pltpu.VMEM((2, rows, width), F32),
            pltpu.VMEM((2, NORM_GROUPS, rows // chans, width), F32),
            pltpu.VMEM((total, chans, width), BF16),
            pltpu.VMEM((total, chans, width), BF16),
            pltpu.SMEM(lengths.shape, jnp.int32),
            pltpu.SemaphoreType.DMA((total // 2,)),
            pltpu.SemaphoreType.DMA((total // 2, 2)),
            pltpu.SemaphoreType.DMA,
        ],
        compiler_params=pltpu.CompilerParams(vmem_limit_bytes=20 * 1024 * 1024),
        cost_estimate=pl.CostEstimate(flops=10_000_000, bytes_accessed=5_000_000, transcendentals=0),
    )(in_hbm(lengths), in_hbm(video), in_hbm(cache))


def in_hbm(value):
    return pltpu.with_memory_space_constraint(value, pltpu.HBM)


def prepare_kernel(first_in_ref, last_in_ref, raw_ref, first_ref, last_ref, weight_ref):
    chans = raw_ref.shape[0]
    for b in range(3):
        for a in range(3):
            for e in range(3):
                source = ((a * 3 + b) * 3 + e) * chans
                column = (b * 3 + a) * chans
                weight_ref[e * chans : (e + 1) * chans, column : column + chans] = raw_ref[:, source : source + chans]


def prepare(first, last, weight):
    chans = weight.shape[0]
    vmem = pl.BlockSpec(memory_space=pltpu.VMEM)
    hbm = pl.BlockSpec(memory_space=pl.ANY)
    return pl.pallas_call(
        prepare_kernel,
        in_specs=[hbm, hbm, vmem],
        out_specs=[hbm, hbm, vmem],
        out_shape=[
            pltpu.HBM(first.shape, BF16),
            pltpu.HBM(last.shape, BF16),
            jax.ShapeDtypeStruct((3 * chans, 9 * chans), BF16),
        ],
        input_output_aliases={0: 0, 1: 1},
        compiler_params=pltpu.CompilerParams(vmem_limit_bytes=16 * 1024 * 1024),
        cost_estimate=pl.CostEstimate(flops=6_000_000_000, bytes_accessed=20_000_000, transcendentals=0),
    )(in_hbm(first), in_hbm(last), weight)


def fill_norm(stats_ref, lengths_ref, norm_ref):
    _, chans, width = norm_ref.shape
    strips, groups2 = stats_ref.shape
    per_group = chans // NORM_GROUPS
    height = 8
    count = (lengths_ref[lax.axis_index("grp")] * (per_group * height * strips * width)).astype(F32)
    row = jnp.sum(stats_ref[...], axis=0, keepdims=True) * jnp.ones((chans, 1), F32) / count
    lane = lax.broadcasted_iota(jnp.int32, (chans, groups2), 1)
    group = lax.broadcasted_iota(jnp.int32, (chans, groups2), 0) // per_group
    mean = jnp.sum(jnp.where(lane == group, row, 0.0), axis=1, keepdims=True)
    square = jnp.sum(jnp.where(lane == group + NORM_GROUPS, row, 0.0), axis=1, keepdims=True)
    scale = 0.5 * lax.rsqrt(square - mean * mean + epsilon)
    norm_ref[0] = jnp.broadcast_to(scale, (chans, width))
    norm_ref[1] = jnp.broadcast_to(-mean * scale, (chans, width))


def shift_sum(y, chans, width):
    outs = []
    lane = lax.broadcasted_iota(jnp.int32, (chans, width), 1)
    for f in range(y.shape[1] // width):
        part = slice(f * width, (f + 1) * width)
        left = pltpu.roll(y[0:chans, part], 1, 1)
        right = pltpu.roll(y[2 * chans : 3 * chans, part], width - 1, 1)
        outs.append(
            y[chans : 2 * chans, part] + jnp.where(lane > 0, left, 0.0) + jnp.where(lane < width - 1, right, 0.0)
        )
    return outs


def project(latent, mixed):
    latent2 = jnp.concatenate([latent, latent], axis=1)
    value = jnp.concatenate(mixed, axis=1)
    high = value.astype(BF16)
    low = (value - high.astype(F32)).astype(BF16)
    return jnp.dot(latent2, jnp.concatenate([high, low], axis=0), preferred_element_type=F32)


def conv_kernel(
    lengths_ref, stats_ref, video_ref, cache_ref, weight_ref, latent_ref, lat_ref, edge_ref,
    seq_ref, rows_ref, norm_ref, sems, *buffers,
):
    pair, height, chans, width = buffers[0].shape
    total = seq_ref.shape[0]
    pairs = total // 2
    held, owns = buffers[:3], buffers[3:]
    deep = 3 * chans
    order = [list(range(1, 4)), list(range(4, 7)), [0], [height - 1]]

    def fetch(p):
        return pltpu.make_async_copy(video_ref.at[pl.ds(2 * p - 2, 2)], seq_ref.at[pl.ds(2 * p, 2)], sems.at[p])

    def fetch_cache():
        return pltpu.make_async_copy(cache_ref, seq_ref.at[pl.ds(0, 2)], sems.at[0])

    fetch_cache().start()
    for p in range(1, pairs):
        fetch(p).start()
    fill_norm(stats_ref, lengths_ref, norm_ref)

    def widen(p):
        for j in range(pair):
            rows_ref[j] = seq_ref[2 * p + j].astype(F32)

    def turn(j, r):
        return rows_ref[j, pl.ds(r, chans, stride=height), :]

    def activate(k, r):
        for j in range(pair):
            x = turn(j, r)
            owns[k % 3][j, r] = x.astype(BF16)
            held[k % 3][j, r] = half_silu(x * norm_ref[0] + norm_ref[1]).astype(BF16)

    fetch_cache().wait()
    widen(0)
    for r in range(height):
        for j in range(pair):
            held[0][j, r] = turn(j, r).astype(BF16)
    fetch(1).wait()
    widen(1)
    for r in range(height):
        activate(1, r)

    def taps_of(r):
        return [b for b in range(3) if 0 <= r + b - 1 < height]

    def step(p, k, more):
        before, now, own_ref = held[(k - 1) % 3], held[k % 3], owns[k % 3]
        if more:
            fetch(p + 1).wait()
            widen(p + 1)

        def multiply(rows):
            taps = taps_of(rows[0])
            columns = []
            for r in rows:
                for f in range(pair):
                    blocks = []
                    for b in taps:
                        for a in range(3):
                            source = before if f + a < 2 else now
                            blocks.append(source[(f + a) % 2, r + b - 1])
                    columns.append(jnp.concatenate(blocks, axis=0))
            x = jnp.concatenate(columns, axis=1)
            return jnp.dot(weight_ref[:, taps[0] * deep : (taps[-1] + 1) * deep], x, preferred_element_type=F32)

        def mix(rows, y):
            conv = shift_sum(y, chans, width)
            places = [(r, f) for r in rows for f in range(pair)]
            mixed = [conv[i] + own_ref[f, r].astype(F32) for i, (r, f) in enumerate(places)]
            if rows[0] == 0 or rows[0] == height - 1:
                for m, (r, f) in zip(mixed, places):
                    edge_ref[2 * p - 2 + f, 0 if r == 0 else 1] = m
                return None
            return [half_silu(0.5 * m) for m in mixed]

        def write(rows, mixed):
            latent = project(latent_ref[...], mixed)
            places = [(r, f) for r in rows for f in range(pair)]
            for i, (r, f) in enumerate(places):
                lat_ref[2 * p - 2 + f, pl.ds(r, latent.shape[0], stride=height), :] = latent[:, i * width : (i + 1) * width]

        to_mix, to_write = [], []
        to_activate = list(range(height)) if more else []
        for rows in order:
            y = multiply(rows)
            if to_mix:
                done, its = to_mix.pop(0)
                mixed = mix(done, its)
                if mixed is not None:
                    to_write.append((done, mixed))
            for _ in range(-(-height // len(order))):
                if to_activate:
                    activate(k + 1, to_activate.pop(0))
            if len(to_write) > 1:
                write(*to_write.pop(0))
            to_mix.append((rows, y))
        for done, its in to_mix:
            mixed = mix(done, its)
            if mixed is not None:
                to_write.append((done, mixed))
        for item in to_write:
            write(*item)

    def steps(i, carry):
        for k in range(1, 4):
            step(3 * i + k, k, True)
        return carry

    turns = (pairs - 2) // 3
    lax.fori_loop(0, turns, steps, 0)
    for p in range(3 * turns + 1, pairs):
        step(p, p, p + 1 < pairs)


def convolve(lengths, stats, video, cache, weight, latent):
    frames, rows, width = video.shape
    chans = weight.shape[0] // 3
    height = rows // chans
    total = frames + 2
    lat = latent.shape[0]
    vmem = pl.BlockSpec(memory_space=pltpu.VMEM)
    hbm = pl.BlockSpec(memory_space=pl.ANY)
    return pl.pallas_call(
        conv_kernel,
        in_specs=[pl.BlockSpec(memory_space=pltpu.SMEM), vmem, hbm, hbm, vmem, vmem],
        out_specs=[vmem, vmem],
        out_shape=[
            jax.ShapeDtypeStruct((frames, lat * height, width), F32),
            jax.ShapeDtypeStruct((frames, 2, chans, width), F32),
        ],
        scratch_shapes=[
            pltpu.VMEM((total, rows, width), BF16),
            pltpu.VMEM((2, rows, width), F32),
            pltpu.VMEM((2, chans, width), F32),
            pltpu.SemaphoreType.DMA((total // 2,)),
        ]
        + [pltpu.VMEM((2, height, chans, width), BF16)] * 6,
        compiler_params=pltpu.CompilerParams(vmem_limit_bytes=24 * 1024 * 1024),
        cost_estimate=pl.CostEstimate(flops=13_000_000_000, bytes_accessed=14_000_000, transcendentals=4_000_000),
    )(lengths, stats, in_hbm(video), in_hbm(cache), weight, latent)


def finish_kernel(
    lengths_ref, stats_ref, above_ref, below_ref, weight_ref, latent_ref, lat_ref, edge_ref, out_ref,
    norm_ref, halo_ref, rows_ref, done_ref, sems,
):
    total, chans, width = above_ref.shape
    frames = total - 2
    lat = latent_ref.shape[0]
    height = lat_ref.shape[1] // lat
    deep = 3 * chans
    length = lengths_ref[lax.axis_index("grp")]
    strip = lax.axis_index("sp")
    inside = ((strip > 0).astype(F32), (strip < lax.axis_size("sp") - 1).astype(F32))
    halos = (above_ref, below_ref)
    fill_norm(stats_ref, lengths_ref, norm_ref)

    def activate(t):
        for side in range(2):
            value = halos[side][t].astype(F32)
            if t >= 2:
                value = half_silu(value * norm_ref[0] + norm_ref[1])
            halo_ref[side, t] = (value * inside[side]).astype(BF16)

    def multiply(side, p):
        columns = [jnp.concatenate([halo_ref[side, 4 * p + f + a] for a in range(3)], axis=0) for f in range(4)]
        return jnp.dot(
            weight_ref[:, 2 * side * deep : (2 * side + 1) * deep], jnp.concatenate(columns, axis=1), preferred_element_type=F32
        )

    def mix(side, p, y):
        conv = shift_sum(y, chans, width)
        return [half_silu(0.5 * (conv[f] + edge_ref[4 * p + f, side])) for f in range(4)]

    def write(side, p, mixed):
        latent = project(latent_ref[...], mixed)
        for f in range(4):
            rows_ref[4 * p + f, pl.ds(side * (height - 1), lat, stride=height), :] = latent[:, f * width : (f + 1) * width]

    def put(p):
        for t in range(4 * p, 4 * p + 4):
            live = (t < length).astype(F32)
            done_ref[t] = (rows_ref[t] * live).astype(BF16)
        leave(p).start()

    def leave(p):
        return pltpu.make_async_copy(done_ref.at[pl.ds(4 * p, 4)], out_ref.at[pl.ds(4 * p, 4)], sems.at[p])

    for t in range(6):
        activate(t)
    to_mix, to_write = [], []
    for p in range(frames // 4):
        for side in range(2):
            y = multiply(side, p)
            if side == 0:
                rows_ref[4 * p : 4 * p + 4] = lat_ref[4 * p : 4 * p + 4]
                for t in (4 * p + 6, 4 * p + 7):
                    if t < total:
                        activate(t)
            else:
                for t in (4 * p + 8, 4 * p + 9):
                    if t < total:
                        activate(t)
            if to_mix:
                before = to_mix.pop(0)
                to_write.append(before[:2] + (mix(*before),))
            if len(to_write) > 1:
                done = to_write.pop(0)
                write(*done)
                if done[0] == 1:
                    put(done[1])
            to_mix.append((side, p, y))
    for item in to_mix:
        to_write.append(item[:2] + (mix(*item),))
    for item in to_write:
        write(*item)
        if item[0] == 1:
            put(item[1])
    for p in range(frames // 4):
        leave(p).wait()


def finish(lengths, stats, above, below, weight, latent, lat_rows, edge):
    total, chans, width = above.shape
    frames = total - 2
    vmem = pl.BlockSpec(memory_space=pltpu.VMEM)
    return pl.pallas_call(
        finish_kernel,
        in_specs=[pl.BlockSpec(memory_space=pltpu.SMEM)] + [vmem] * 7,
        out_specs=pl.BlockSpec(memory_space=pl.ANY),
        out_shape=pltpu.HBM(lat_rows.shape, BF16),
        scratch_shapes=[
            pltpu.VMEM((2, chans, width), F32),
            pltpu.VMEM((2, total, chans, width), BF16),
            pltpu.VMEM(lat_rows.shape, F32),
            pltpu.VMEM(lat_rows.shape, BF16),
            pltpu.SemaphoreType.DMA((frames // 2,)),
        ],
        compiler_params=pltpu.CompilerParams(vmem_limit_bytes=20 * 1024 * 1024),
        cost_estimate=pl.CostEstimate(flops=1_300_000_000, bytes_accessed=6_000_000, transcendentals=1_000_000),
    )(lengths, stats, above, below, weight, latent, lat_rows, edge)


def body(video, cache, conv_weight, latent_weight, clip_lengths):
    _, frames, chans, height, width = video.shape
    video = video.reshape(frames, chans * height, width)
    cache = cache.reshape(2, chans * height, width)
    strips = lax.axis_size("sp")
    first, last, stats = stage(clip_lengths, video, cache, chans, strips)
    stats = lax.all_to_all(stats, "sp", split_axis=0, concat_axis=0, tiled=True)
    first, last, weight = prepare(first, last, conv_weight)
    above = lax.ppermute(last, "sp", [(i, i + 1) for i in range(strips - 1)])
    below = lax.ppermute(first, "sp", [(i + 1, i) for i in range(strips - 1)])
    lat_rows, edge = convolve(clip_lengths, stats, video, cache, weight, latent_weight)
    out = finish(clip_lengths, stats, above, below, weight, latent_weight, lat_rows, edge)
    return out.reshape(1, frames, latent_weight.shape[0], height, width)


def solution(mesh):
    in_specs = (P("grp", None, None, "sp", None), P("grp", None, None, "sp", None), P(), P(), P())
    out_specs = P("grp", None, None, "sp", None)
    return jax.shard_map(body, mesh=mesh, in_specs=in_specs, out_specs=out_specs, check_vma=False)
```

```python
import functools

import jax
import jax.numpy as jnp
from jax import lax
from jax.experimental import pallas as pl
from jax.experimental.pallas import tpu as pltpu
from jax.sharding import PartitionSpec as P

NORM_GROUPS = 32
epsilon = 1e-06
F32 = jnp.float32
BF16 = jnp.bfloat16


def half_silu(u):
    return u + u * jnp.tanh(u)


def stage_kernel(
    lengths_ref, video_ref, cache_ref, first_out_ref, last_out_ref, stats_ref,
    held_ref, rows_ref, acc_ref, first_ref, last_ref, table_ref, sems, out_sems, table_sem,
):
    total, chans, width = first_ref.shape
    height = video_ref.shape[1] // chans
    per_group = chans // NORM_GROUPS
    part = 16
    table = pltpu.make_async_copy(lengths_ref, table_ref, table_sem)
    table.start()

    def fetch(p):
        return pltpu.make_async_copy(video_ref.at[pl.ds(2 * p - 2, 2)], held_ref.at[pl.ds(2 * p, 2)], sems.at[p])

    def fetch_cache():
        return pltpu.make_async_copy(cache_ref, held_ref.at[pl.ds(0, 2)], sems.at[0])

    def leave(p, side):
        held, out = ((first_ref, first_out_ref), (last_ref, last_out_ref))[side]
        return pltpu.make_async_copy(held.at[pl.ds(2 * p, 2)], out.at[pl.ds(2 * p, 2)], out_sems.at[p, side])

    for p in range(1, total // 2):
        fetch(p).start()
    fetch_cache().start()
    acc_ref[...] = jnp.zeros_like(acc_ref)
    table.wait()
    length = table_ref[lax.axis_index("grp")]

    def turn(j, t, live):
        for k in range(chans // part):
            rows = slice(k * part * height, (k + 1) * part * height)
            x = held_ref[t, rows].astype(F32)
            rows_ref[j, rows] = x
            if live is not None:
                some = slice(k * part // per_group, (k + 1) * part // per_group)
                grouped = x.reshape(part // per_group, per_group, height, width)
                acc_ref[0, some] += jnp.sum(grouped, axis=1) * live
                acc_ref[1, some] += jnp.sum(grouped * grouped, axis=1) * live
        first_ref[t] = rows_ref[j, pl.ds(0, chans, stride=height), :].astype(BF16)
        last_ref[t] = rows_ref[j, pl.ds(height - 1, chans, stride=height), :].astype(BF16)

    def pair(p, carry):
        fetch(p).wait()
        for j in range(2):
            turn(j, 2 * p + j, (2 * p - 2 + j < length).astype(F32))
        for side in range(2):
            leave(p, side).start()
        return carry

    lax.fori_loop(1, total // 2, pair, 0)
    fetch_cache().wait()
    for j in range(2):
        turn(j, j, None)
    for side in range(2):
        leave(0, side).start()
    partial = jnp.sum(acc_ref[...], axis=2).reshape(2 * NORM_GROUPS, width)
    stats_ref[...] = lax.dot_general(
        jnp.ones((stats_ref.shape[0], width), F32), partial, (((1,), (1,)), ((), ())),
        precision=lax.Precision.HIGHEST, preferred_element_type=F32,
    )
    for p in range(total // 2):
        for side in range(2):
            leave(p, side).wait()


def stage(lengths, video, cache, chans, copies):
    frames, rows, width = video.shape
    total = frames + 2
    vmem = pl.BlockSpec(memory_space=pltpu.VMEM)
    hbm = pl.BlockSpec(memory_space=pl.ANY)
    return pl.pallas_call(
        stage_kernel,
        in_specs=[hbm, hbm, hbm],
        out_specs=[hbm, hbm, vmem],
        out_shape=[
            pltpu.HBM((total, chans, width), BF16),
            pltpu.HBM((total, chans, width), BF16),
            jax.ShapeDtypeStruct((copies, 2 * NORM_GROUPS), F32),
        ],
        scratch_shapes=[
            pltpu.VMEM((total, rows, width), BF16),
            pltpu.VMEM((2, rows, width), F32),
            pltpu.VMEM((2, NORM_GROUPS, rows // chans, width), F32),
            pltpu.VMEM((total, chans, width), BF16),
            pltpu.VMEM((total, chans, width), BF16),
            pltpu.SMEM(lengths.shape, jnp.int32),
            pltpu.SemaphoreType.DMA((total // 2,)),
            pltpu.SemaphoreType.DMA((total // 2, 2)),
            pltpu.SemaphoreType.DMA,
        ],
        compiler_params=pltpu.CompilerParams(vmem_limit_bytes=20 * 1024 * 1024),
        cost_estimate=pl.CostEstimate(flops=10_000_000, bytes_accessed=5_000_000, transcendentals=0),
    )(in_hbm(lengths), in_hbm(video), in_hbm(cache))


def in_hbm(value):
    return pltpu.with_memory_space_constraint(value, pltpu.HBM)


def prepare_kernel(first_in_ref, last_in_ref, raw_ref, first_ref, last_ref, weight_ref):
    chans = raw_ref.shape[0]
    for b in range(3):
        for a in range(3):
            for e in range(3):
                source = ((a * 3 + b) * 3 + e) * chans
                column = (b * 3 + a) * chans
                weight_ref[e * chans : (e + 1) * chans, column : column + chans] = raw_ref[:, source : source + chans]


def prepare(first, last, weight):
    chans = weight.shape[0]
    vmem = pl.BlockSpec(memory_space=pltpu.VMEM)
    hbm = pl.BlockSpec(memory_space=pl.ANY)
    return pl.pallas_call(
        prepare_kernel,
        in_specs=[hbm, hbm, vmem],
        out_specs=[hbm, hbm, vmem],
        out_shape=[
            pltpu.HBM(first.shape, BF16),
            pltpu.HBM(last.shape, BF16),
            jax.ShapeDtypeStruct((3 * chans, 9 * chans), BF16),
        ],
        input_output_aliases={0: 0, 1: 1},
        compiler_params=pltpu.CompilerParams(vmem_limit_bytes=16 * 1024 * 1024),
        cost_estimate=pl.CostEstimate(flops=6_000_000_000, bytes_accessed=20_000_000, transcendentals=0),
    )(in_hbm(first), in_hbm(last), weight)


def fill_norm(stats_ref, lengths_ref, norm_ref):
    _, chans, width = norm_ref.shape
    strips, groups2 = stats_ref.shape
    per_group = chans // NORM_GROUPS
    height = 8
    count = (lengths_ref[lax.axis_index("grp")] * (per_group * height * strips * width)).astype(F32)
    row = jnp.sum(stats_ref[...], axis=0, keepdims=True) * jnp.ones((chans, 1), F32) / count
    lane = lax.broadcasted_iota(jnp.int32, (chans, groups2), 1)
    group = lax.broadcasted_iota(jnp.int32, (chans, groups2), 0) // per_group
    mean = jnp.sum(jnp.where(lane == group, row, 0.0), axis=1, keepdims=True)
    square = jnp.sum(jnp.where(lane == group + NORM_GROUPS, row, 0.0), axis=1, keepdims=True)
    scale = 0.5 * lax.rsqrt(square - mean * mean + epsilon)
    norm_ref[0] = jnp.broadcast_to(scale, (chans, width))
    norm_ref[1] = jnp.broadcast_to(-mean * scale, (chans, width))


def shift_sum(y, chans, width):
    outs = []
    lane = lax.broadcasted_iota(jnp.int32, (chans, width), 1)
    for f in range(y.shape[1] // width):
        part = slice(f * width, (f + 1) * width)
        left = pltpu.roll(y[0:chans, part], 1, 1)
        right = pltpu.roll(y[2 * chans : 3 * chans, part], width - 1, 1)
        outs.append(
            y[chans : 2 * chans, part] + jnp.where(lane > 0, left, 0.0) + jnp.where(lane < width - 1, right, 0.0)
        )
    return outs


def project(latent, mixed):
    latent2 = jnp.concatenate([latent, latent], axis=1)
    value = jnp.concatenate(mixed, axis=1)
    high = value.astype(BF16)
    low = (value - high.astype(F32)).astype(BF16)
    return jnp.dot(latent2, jnp.concatenate([high, low], axis=0), preferred_element_type=F32)


def conv_kernel(
    lengths_ref, stats_ref, video_ref, cache_ref, weight_ref, latent_ref, lat_ref, edge_ref,
    seq_ref, rows_ref, norm_ref, sems, *buffers,
):
    pair, height, chans, width = buffers[0].shape
    total = seq_ref.shape[0]
    pairs = total // 2
    held, owns = buffers[:3], buffers[3:]
    deep = 3 * chans
    order = [list(range(1, 4)), list(range(4, 7)), [0], [height - 1]]

    def fetch(p):
        return pltpu.make_async_copy(video_ref.at[pl.ds(2 * p - 2, 2)], seq_ref.at[pl.ds(2 * p, 2)], sems.at[p])

    def fetch_cache():
        return pltpu.make_async_copy(cache_ref, seq_ref.at[pl.ds(0, 2)], sems.at[0])

    fetch_cache().start()
    for p in range(1, pairs):
        fetch(p).start()
    fill_norm(stats_ref, lengths_ref, norm_ref)

    def widen(p):
        for j in range(pair):
            rows_ref[j] = seq_ref[2 * p + j].astype(F32)

    def turn(j, r):
        return rows_ref[j, pl.ds(r, chans, stride=height), :]

    def activate(k, r):
        for j in range(pair):
            x = turn(j, r)
            owns[k % 3][j, r] = x.astype(BF16)
            held[k % 3][j, r] = half_silu(x * norm_ref[0] + norm_ref[1]).astype(BF16)

    fetch_cache().wait()
    widen(0)
    for r in range(height):
        for j in range(pair):
            held[0][j, r] = turn(j, r).astype(BF16)
    fetch(1).wait()
    widen(1)
    for r in range(height):
        activate(1, r)

    def taps_of(r):
        return [b for b in range(3) if 0 <= r + b - 1 < height]

    def step(p, k, more):
        before, now, own_ref = held[(k - 1) % 3], held[k % 3], owns[k % 3]
        if more:
            fetch(p + 1).wait()
            widen(p + 1)

        def multiply(rows):
            taps = taps_of(rows[0])
            columns = []
            for r in rows:
                for f in range(pair):
                    blocks = []
                    for b in taps:
                        for a in range(3):
                            source = before if f + a < 2 else now
                            blocks.append(source[(f + a) % 2, r + b - 1])
                    columns.append(jnp.concatenate(blocks, axis=0))
            x = jnp.concatenate(columns, axis=1)
            return jnp.dot(weight_ref[:, taps[0] * deep : (taps[-1] + 1) * deep], x, preferred_element_type=F32)

        def mix(rows, y):
            conv = shift_sum(y, chans, width)
            places = [(r, f) for r in rows for f in range(pair)]
            mixed = [conv[i] + own_ref[f, r].astype(F32) for i, (r, f) in enumerate(places)]
            if rows[0] == 0 or rows[0] == height - 1:
                for m, (r, f) in zip(mixed, places):
                    edge_ref[2 * p - 2 + f, 0 if r == 0 else 1] = m
                return None
            return [half_silu(0.5 * m) for m in mixed]

        def write(rows, mixed):
            latent = project(latent_ref[...], mixed)
            places = [(r, f) for r in rows for f in range(pair)]
            for i, (r, f) in enumerate(places):
                lat_ref[2 * p - 2 + f, pl.ds(r, latent.shape[0], stride=height), :] = latent[:, i * width : (i + 1) * width]

        to_mix, to_write = [], []
        to_activate = list(range(height)) if more else []
        for rows in order:
            y = multiply(rows)
            if to_mix:
                done, its = to_mix.pop(0)
                mixed = mix(done, its)
                if mixed is not None:
                    to_write.append((done, mixed))
            for _ in range(-(-height // len(order))):
                if to_activate:
                    activate(k + 1, to_activate.pop(0))
            if len(to_write) > 1:
                write(*to_write.pop(0))
            to_mix.append((rows, y))
        for done, its in to_mix:
            mixed = mix(done, its)
            if mixed is not None:
                to_write.append((done, mixed))
        for item in to_write:
            write(*item)

    def steps(i, carry):
        for k in range(1, 4):
            step(3 * i + k, k, True)
        return carry

    turns = (pairs - 2) // 3
    lax.fori_loop(0, turns, steps, 0)
    for p in range(3 * turns + 1, pairs):
        step(p, p, p + 1 < pairs)


def convolve(lengths, stats, video, cache, weight, latent):
    frames, rows, width = video.shape
    chans = weight.shape[0] // 3
    height = rows // chans
    total = frames + 2
    lat = latent.shape[0]
    vmem = pl.BlockSpec(memory_space=pltpu.VMEM)
    hbm = pl.BlockSpec(memory_space=pl.ANY)
    return pl.pallas_call(
        conv_kernel,
        in_specs=[pl.BlockSpec(memory_space=pltpu.SMEM), vmem, hbm, hbm, vmem, vmem],
        out_specs=[vmem, vmem],
        out_shape=[
            jax.ShapeDtypeStruct((frames, lat * height, width), F32),
            jax.ShapeDtypeStruct((frames, 2, chans, width), F32),
        ],
        scratch_shapes=[
            pltpu.VMEM((total, rows, width), BF16),
            pltpu.VMEM((2, rows, width), F32),
            pltpu.VMEM((2, chans, width), F32),
            pltpu.SemaphoreType.DMA((total // 2,)),
        ]
        + [pltpu.VMEM((2, height, chans, width), BF16)] * 6,
        compiler_params=pltpu.CompilerParams(vmem_limit_bytes=24 * 1024 * 1024),
        cost_estimate=pl.CostEstimate(flops=13_000_000_000, bytes_accessed=14_000_000, transcendentals=4_000_000),
    )(lengths, stats, in_hbm(video), in_hbm(cache), weight, latent)


def finish_kernel(
    side, final, lengths_ref, stats_ref, row_ref, weight_ref, latent_ref, lat_ref, edge_ref, out_ref,
    norm_ref, halo_ref, *scratch,
):
    total, chans, width = row_ref.shape
    frames = total - 2
    lat = latent_ref.shape[0]
    height = lat_ref.shape[1] // lat
    deep = 3 * chans
    length = lengths_ref[lax.axis_index("grp")]
    strip = lax.axis_index("sp")
    inside = (strip < lax.axis_size("sp") - 1 if side else strip > 0).astype(F32)
    fill_norm(stats_ref, lengths_ref, norm_ref)

    def activate(t):
        value = row_ref[t].astype(F32)
        if t >= 2:
            value = half_silu(value * norm_ref[0] + norm_ref[1])
        halo_ref[t] = (value * inside).astype(BF16)

    def multiply(p):
        columns = [jnp.concatenate([halo_ref[2 * p + f + a] for a in range(3)], axis=0) for f in range(2)]
        return jnp.dot(
            weight_ref[:, 2 * side * deep : (2 * side + 1) * deep], jnp.concatenate(columns, axis=1), preferred_element_type=F32
        )

    def mix(p, y):
        conv = shift_sum(y, chans, width)
        return [half_silu(0.5 * (conv[f] + edge_ref[2 * p + f, side])) for f in range(2)]

    def write(p, mixed):
        latent = project(latent_ref[...], mixed)
        rows_ref = scratch[0] if final else out_ref
        for f in range(2):
            t = 2 * p + f
            rows_ref[t, pl.ds(side * (height - 1), lat, stride=height), :] = latent[:, f * width : (f + 1) * width]
            if final:
                live = (t < length).astype(F32)
                out_ref[t] = (rows_ref[t] * live).reshape(lat, height, width).astype(BF16)

    if final:
        scratch[0][...] = lat_ref[...]
    else:
        out_ref[...] = lat_ref[...]
    for t in range(4):
        activate(t)
    to_mix, to_write = [], []
    for p in range(frames // 2):
        y = multiply(p)
        for t in (2 * p + 4, 2 * p + 5):
            if t < total:
                activate(t)
        if to_mix:
            before = to_mix.pop(0)
            to_write.append((before[0], mix(*before)))
        if len(to_write) > 1:
            write(*to_write.pop(0))
        to_mix.append((p, y))
    for item in to_mix:
        to_write.append((item[0], mix(*item)))
    for item in to_write:
        write(*item)


def finish(side, final, lengths, stats, row, weight, latent, lat_rows, edge):
    total, chans, width = row.shape
    frames = total - 2
    lat = latent.shape[0]
    height = lat_rows.shape[1] // lat
    vmem = pl.BlockSpec(memory_space=pltpu.VMEM)
    scratch = [pltpu.VMEM((2, chans, width), F32), pltpu.VMEM((total, chans, width), BF16)]
    if final:
        out = jax.ShapeDtypeStruct((frames, lat, height, width), BF16)
        scratch.append(pltpu.VMEM(lat_rows.shape, F32))
    else:
        out = jax.ShapeDtypeStruct(lat_rows.shape, F32)
    return pl.pallas_call(
        functools.partial(finish_kernel, side, final),
        in_specs=[pl.BlockSpec(memory_space=pltpu.SMEM)] + [vmem] * 6,
        out_specs=vmem,
        out_shape=out,
        scratch_shapes=scratch,
        compiler_params=pltpu.CompilerParams(vmem_limit_bytes=20 * 1024 * 1024),
        cost_estimate=pl.CostEstimate(flops=700_000_000, bytes_accessed=3_000_000, transcendentals=500_000),
    )(lengths, stats, row, weight, latent, lat_rows, edge)


def body(video, cache, conv_weight, latent_weight, clip_lengths):
    _, frames, chans, height, width = video.shape
    video = video.reshape(frames, chans * height, width)
    cache = cache.reshape(2, chans * height, width)
    strips = lax.axis_size("sp")
    first, last, stats = stage(clip_lengths, video, cache, chans, strips)
    stats = lax.all_to_all(stats, "sp", split_axis=0, concat_axis=0, tiled=True)
    first, last, weight = prepare(first, last, conv_weight)
    above = lax.ppermute(last, "sp", [(i, i + 1) for i in range(strips - 1)])
    stats, first = lax.optimization_barrier((stats, first))
    below = lax.ppermute(first, "sp", [(i + 1, i) for i in range(strips - 1)])
    lat_rows, edge = convolve(clip_lengths, stats, video, cache, weight, latent_weight)
    lat_rows = finish(0, False, clip_lengths, stats, above, weight, latent_weight, lat_rows, edge)
    out = finish(1, True, clip_lengths, stats, below, weight, latent_weight, lat_rows, edge)
    return out[None]


def solution(mesh):
    in_specs = (P("grp", None, None, "sp", None), P("grp", None, None, "sp", None), P(), P(), P())
    out_specs = P("grp", None, None, "sp", None)
    return jax.shard_map(body, mesh=mesh, in_specs=in_specs, out_specs=out_specs, check_vma=False)
```
